32 devices in a mesh: grp: 2 (over y), con: 4 (over z), rep: 2 (over x), sub: 2 (over core).
Axes of the slice: x: 2, y: 2, z: 4, core: 2. Of those that a mesh axis runs over, the one named last changes fastest.
Arguments:
- integrals: float32 [512, 9600], P(('grp', 'con'), ('rep', 'sub')), parts along dimension 0, as said below
- ladder: float32 [19200, 9600], P(('grp', 'con'), ('rep', 'sub')), parts along dimension 0, may hold values from -0.1875 to 0.1875
- pair_energy: float32 [512], P(('grp', 'con')), parts along dimension 0, may hold values from -3 to -1
- virt_energy: float32 [19200], P(('grp', 'rep', 'sub')), parts along dimension 0, may hold values from 0.5 to 3
- pair_irrep: int32 [512], P('grp'), parts along dimension 0, may hold values from 0 to 7, as said below
- virt_irrep: int32 [19200], P('grp'), parts along dimension 0, may hold values from 0 to 7, as said below
Outputs:
- amplitude: float32 [512, 9600], P(('grp', 'con'), ('rep', 'sub')), parts along dimension 0
The draws below stay inside these ranges and needn't reach their ends.
There are 2 independent parts, one for each index of `grp`. The reference program is written for one: setup_inputs(seed, part) draws one part's arguments, and reference() takes and returns one part's arrays. A program takes and returns all parts, laid end to end along the dimension named above; each array names one. Nothing has to cross between parts.
Inputs may be any that keep to these rules, and one draw needn't show every extreme that they name: `pair_irrep`: sorted ascending; the rows of one label form one run of at most 48 rows, and some label has exactly 48. `virt_irrep`: sorted ascending within each aligned block of 2400 virtual pairs; a label holds at most 600 virtual pairs of a block, and in every block some label holds exactly 600. `integrals`: zero wherever the row's pair_irrep differs from the column's virt_irrep.
All inputs are finite; a program needn't handle non-finite values.
Results may differ from the reference program's by a relative error of at most 0.0001.
Values sent between devices are 32-bit elements; how exact they have to be, the bound alone decides.
A program may use at most 192 MiB of HBM per device.

```python
import jax
import jax.numpy as jnp
from jax import lax

ITERS = 2
PAIRS = 256
KV = 9600
VBLOCK = 2400


def run_labels(key, count, pattern, unit):
    lengths = jax.random.permutation(key, jnp.array(pattern, dtype=jnp.int32)) * unit
    ends = jnp.cumsum(lengths)
    position = jnp.arange(count, dtype=jnp.int32)
    return jnp.sum((position[:, None] >= ends[None, :]).astype(jnp.int32), axis=1)


def pair_labels(key):
    return run_labels(jax.random.fold_in(key, 11), PAIRS, [3, 3, 2, 2, 2, 2, 1, 1], PAIRS // 16)


def virt_labels(key):
    block_keys = jax.random.split(jax.random.fold_in(key, 12), KV // VBLOCK)
    blocks = jax.vmap(lambda one_key: run_labels(one_key, VBLOCK, [2, 1, 1, 1, 1, 1, 1, 0], VBLOCK // 8))(block_keys)
    return blocks.reshape(KV)


def draw_pair_irrep(key, part):
    return pair_labels(key)


def draw_virt_irrep(key, part):
    return virt_labels(key)


def draw_integrals(key, part):
    row_labels = pair_labels(key)
    col_labels = virt_labels(key)
    key = jax.random.fold_in(key, 3)
    values = jnp.clip(jax.random.normal(key, (PAIRS, KV), jnp.float32), -6.0, 6.0)
    matched = row_labels[:, None] == col_labels[None, :]
    return jnp.where(matched, values, jnp.zeros_like(values)).astype(jnp.float32)


def shard_levels(key, shape, cuts, smallest, high):
    level = 1.0
    for dim, blocks in cuts:
        steps = jax.random.uniform(jax.random.fold_in(jax.random.fold_in(key, 6), dim), (blocks,), jnp.float32, smallest / len(cuts), high / len(cuts))
        level = level * jnp.repeat(jnp.exp(steps), shape[dim] // blocks).reshape((-1,) + (1,) * (len(shape) - 1 - dim))
    return level


def noise(key, extent, deviation, most, shards=(), kind=jnp.bfloat16):
    values = jax.random.normal(key, extent, jnp.float32) * deviation
    if len(shards) > 0:
        values = shard_levels(key, extent, shards, -0.22, 0.18) * values
    return jnp.clip(values, min=-most, max=most).astype(kind)


def setup_inputs(seed: int = 0, part: int = 0) -> dict:
    streams_of = jax.random.split(jax.random.key(seed), 7)
    part_keys = jax.random.split(jax.random.fold_in(streams_of[6], part), 7)
    return {
        "integrals": draw_integrals(jax.random.fold_in(jax.random.fold_in(streams_of[6], part), 71), part),
        "ladder": noise(part_keys[1], (KV, KV), (KV // 8) ** -0.5, 0.1875, ((0, 4), (1, 4)), jnp.float32),
        "pair_energy": jnp.clip(-3.0 + 2.0 * jax.random.uniform(part_keys[2], (PAIRS,), jnp.float32) ** shard_levels(part_keys[2], (PAIRS,), ((0, 4),), -0.2, 0.2), -3.0, -1.0),
        "virt_energy": jnp.clip(0.5 + 2.5 * jax.random.uniform(part_keys[3], (KV,), jnp.float32) ** shard_levels(part_keys[3], (KV,), ((0, 4),), -0.2, 0.2), 0.5, 3.0),
        "pair_irrep": draw_pair_irrep(jax.random.fold_in(jax.random.fold_in(streams_of[6], part), 71), part),
        "virt_irrep": draw_virt_irrep(jax.random.fold_in(jax.random.fold_in(streams_of[6], part), 71), part),
    }


def reference(integrals, ladder, pair_energy, virt_energy, pair_irrep, virt_irrep):
    divisor = virt_energy[None, :] - pair_energy[:, None]
    allowed = pair_irrep[:, None] == virt_irrep[None, :]
    amplitude = integrals / divisor
    for repeat in range(ITERS):
        ladder_term = jnp.dot(amplitude, ladder.T, precision=lax.Precision.HIGHEST, preferred_element_type=jnp.float32)
        amplitude = (integrals + jnp.where(allowed, ladder_term, jnp.zeros_like(ladder_term))) / divisor
    return amplitude
```

```python
import functools

import jax
import jax.numpy as jnp
from jax import lax
from jax.experimental import pallas as pl
from jax.experimental.pallas import tpu as pltpu
from jax.sharding import PartitionSpec as P

ITERS = 2
LABELS = 8
MESH = pl.DeviceIdType.MESH
VMEM = pl.BlockSpec(memory_space=pltpu.VMEM)
SMEM = pl.BlockSpec(memory_space=pltpu.SMEM)


class Dims:
    pass


def take_rows(ref, start, count, *window):
    shift = start % 8
    rows = ref[(*window[:-1], pl.ds(pl.multiple_of(start - shift, 8), count + 8), window[-1])]
    return pltpu.roll(rows, (count + 8 - shift) % (count + 8), 0)[:count]


def pack_kernel(d, tiles, x_ref, label_ref, energy_ref, out_ref, wide):
    for b in range(d.m):
        wide[:, (d.v // 128) * 128 :] = jnp.zeros_like(wide[:, (d.v // 128) * 128 :])
        wide[:, : d.v] = x_ref[:, b * d.v : (b + 1) * d.v]
        value = jnp.zeros((d.rows, d.w), jnp.float32)
        for label in range(LABELS):
            start = pl.multiple_of(tiles[2 + b, label] // 128 * 128, 128)
            value = jnp.where(label_ref[...] == label, wide[:, pl.ds(start, d.w)], value)
        lane = lax.broadcasted_iota(jnp.int32, (d.rows, d.w), 1)
        out_ref[b] = jnp.where(lane == d.w - 1, energy_ref[...], value)


def line_copies(z, n, view, up_send, up_recv, down_send, down_recv):
    def at(t):
        up_block = jnp.maximum(z - t, 0)
        down_block = jnp.minimum(z + t, n - 1)
        up = pltpu.make_async_remote_copy(
            src_ref=view(up_block),
            dst_ref=view(up_block),
            send_sem=up_send.at[t],
            recv_sem=up_recv.at[t],
            device_id={"con": jnp.minimum(z + 1, n - 1)},
            device_id_type=MESH,
        )
        down = pltpu.make_async_remote_copy(
            src_ref=view(down_block),
            dst_ref=view(down_block),
            send_sem=down_send.at[t],
            recv_sem=down_recv.at[t],
            device_id={"con": jnp.maximum(z - 1, 0)},
            device_id_type=MESH,
        )
        return up, down, (z >= t) & (z < n - 1), (z + t <= n - 1) & (z > 0)

    return at


def line_gather(z, n, view, sems, arrived):
    at = line_copies(z, n, view, *sems)
    for t in range(n - 1):
        up, down, can_up, can_down = at(t)
        pl.when(can_up)(up.start)
        pl.when(can_down)(down.start)

        @pl.when(z - 1 - t >= 0)
        def _():
            up.wait_recv()
            arrived(z - 1 - t)

        @pl.when(z + 1 + t <= n - 1)
        def _():
            down.wait_recv()
            arrived(z + 1 + t)

    for t in range(n - 1):
        up, down, can_up, can_down = at(t)
        pl.when(can_up)(up.wait_send)
        pl.when(can_down)(down.wait_send)


def greet(z, n, others):
    barrier = pltpu.get_barrier_semaphore()
    for other in others:
        pl.semaphore_signal(barrier, inc=1, device_id=other, device_id_type=MESH)

    @pl.when(z > 0)
    def _():
        pl.semaphore_signal(barrier, inc=1, device_id={"con": z - 1}, device_id_type=MESH)

    @pl.when(z < n - 1)
    def _():
        pl.semaphore_signal(barrier, inc=1, device_id={"con": z + 1}, device_id_type=MESH)

    near = (z > 0).astype(jnp.int32) + (z < n - 1).astype(jnp.int32)
    pl.semaphore_wait(barrier, near + len(others))


def gather_kernel(d, x_ref, out_ref, *sems):
    z = lax.axis_index("con")
    greet(z, d.con, [])

    def view(block):
        return out_ref.at[:, pl.ds(pl.multiple_of(block * d.rows, 8), d.rows), :]

    out_ref[:, pl.ds(pl.multiple_of(z * d.rows, 8), d.rows), :] = x_ref[...]
    line_gather(z, d.con, view, sems, lambda block: None)


def reduce_kernel(d, x_ref, out_ref, landed, whole, s_send, s_recv, x_send, x_recv, *sems):
    z = lax.axis_index("con")
    j = lax.axis_index("rep") * d.sub + lax.axis_index("sub")

    def device(q):
        return {"rep": q // d.sub, "sub": q % d.sub}

    greet(z, d.con, [device((j + k) % d.rs) for k in range(1, d.rs)])
    copies = []
    for k in range(1, d.rs):
        q = (j + k) % d.rs
        copy = pltpu.make_async_remote_copy(
            src_ref=x_ref.at[q],
            dst_ref=landed.at[k - 1],
            send_sem=s_send.at[k - 1],
            recv_sem=s_recv.at[k - 1],
            device_id=device(q),
            device_id_type=MESH,
        )
        copy.start()
        copies.append(copy)
    total = x_ref[j]
    for k in range(1, d.rs):
        copies[k - 1].wait_recv()
        total = total + landed[k - 1]
    whole[z] = total

    def to_owner(block):
        owner = block // d.m
        return owner, pltpu.make_async_remote_copy(
            src_ref=whole.at[block],
            dst_ref=out_ref.at[block % d.m, j],
            send_sem=x_send.at[block],
            recv_sem=x_recv.at[block % d.m, j],
            device_id=device(owner),
            device_id_type=MESH,
        )

    def arrived(block):
        owner, copy = to_owner(block)
        pl.when(owner != j)(copy.start)

        @pl.when(owner == j)
        def _():
            out_ref[block % d.m, j] = whole[block]

    arrived(z)
    line_gather(z, d.con, lambda block: whole.at[block], sems, arrived)
    for block in range(d.con):
        owner, copy = to_owner(block)
        pl.when(owner != j)(copy.wait_send)
    for b in range(d.m):
        for k in range(1, d.rs):
            q = (j + k) % d.rs
            pltpu.make_async_remote_copy(
                src_ref=whole.at[0],
                dst_ref=out_ref.at[b, q],
                send_sem=x_send.at[0],
                recv_sem=x_recv.at[b, q],
                device_id=device(q),
                device_id_type=MESH,
            ).wait_recv()
    for copy in copies:
        copy.wait_send()


def product(d, info, label_ref, ladder_ref, out_ref, high_low, low, high):
    step = pl.program_id(0)
    row = lax.broadcasted_iota(jnp.int32, (d.cw, d.cols), 0) + step * d.cw
    value = jnp.where((row >= low[...]) & (row < high[...]), ladder_ref[...], 0.0)
    value_high = value.astype(jnp.bfloat16)
    value_low = (value - value_high.astype(jnp.float32)).astype(jnp.bfloat16)
    dims = (((1,), (1,)), ((), ()))
    first = lax.dot_general(value_high, high_low[...], dims, preferred_element_type=jnp.float32)
    second = lax.dot_general(
        value_low, high_low[: d.s, :], dims, preferred_element_type=jnp.float32
    )
    out_ref[0] = jnp.transpose(first[:, : d.s] + first[:, d.s :] + second)


def prepare(d, info, label_ref, amp, high_low, low, high):
    value = amp[...]
    value_high = value.astype(jnp.bfloat16)
    high_low[: d.s, :] = value_high
    high_low[d.s :, :] = (value - value_high.astype(jnp.float32)).astype(jnp.bfloat16)
    first = jnp.zeros((1, d.cols), jnp.int32)
    last = jnp.zeros((1, d.cols), jnp.int32)
    for label in range(LABELS):
        here = label_ref[...] == label
        first = jnp.where(here, info[2 + d.m, label], first)
        last = jnp.where(here, info[3 + d.m, label], last)
    low[...] = first
    high[...] = last


def first_kernel(
    d, info, got_ref, wide_label, wide_energy, label_ref, ladder_ref,
    out_ref, ints_ref, div_ref, amp, high_low, low, high,
):
    @pl.when(pl.program_id(0) == 0)
    def _():
        ints_ref[...] = jnp.zeros_like(ints_ref)
        div_ref[...] = jnp.ones_like(div_ref)
        slot = lax.broadcasted_iota(jnp.int32, (d.s, d.w), 0)
        for b in range(d.m):
            for label in range(LABELS):
                start = pl.multiple_of(info[2 + b, label] // 128 * 128, 128)
                rows = take_rows(got_ref, info[0, label], d.s, b, slice(None))
                window = pl.ds(start, d.w)
                good = (wide_label[b, :, window] == label) & (slot < info[1, label])
                divisor = wide_energy[b, :, window] - rows[:, d.w - 1 : d.w]
                ints_ref[b, :, window] = jnp.where(good, rows, ints_ref[b, :, window])
                div_ref[b, :, window] = jnp.where(good, divisor, div_ref[b, :, window])
            amp[:, b * d.v : (b + 1) * d.v] = ints_ref[b, :, : d.v] / div_ref[b, :, : d.v]
        prepare(d, info, label_ref, amp, high_low, low, high)

    product(d, info, label_ref, ladder_ref, out_ref, high_low, low, high)


def update(d, b, sum_ref, ints_ref, div_ref):
    term = jnp.concatenate([sum_ref[b, q] for q in range(d.rs)], axis=1)
    return (ints_ref[b, :, : d.vp] + term) / div_ref[b, :, : d.vp]


def next_kernel(
    d, info, sum_ref, ints_ref, div_ref, label_ref, ladder_ref, out_ref, amp, high_low, low, high
):
    @pl.when(pl.program_id(0) == 0)
    def _():
        for b in range(d.m):
            amp[:, b * d.v : (b + 1) * d.v] = update(d, b, sum_ref, ints_ref, div_ref)[:, : d.v]
        prepare(d, info, label_ref, amp, high_low, low, high)

    product(d, info, label_ref, ladder_ref, out_ref, high_low, low, high)


def final_kernel(d, info, sum_ref, ints_ref, div_ref, wide_label, row_label, out_ref, slots, wide):
    base = lax.axis_index("con") * d.rows
    for b in range(d.m):
        slots[...] = jnp.zeros_like(slots)
        slots[d.rows : d.rows + d.s, : d.vp] = update(d, b, sum_ref, ints_ref, div_ref)
        wide[...] = jnp.zeros_like(wide)
        for label in range(LABELS):
            start = pl.multiple_of(info[2 + b, label] // 128 * 128, 128)
            window = pl.ds(start, d.w)
            place = jnp.clip(base - info[0, label] + d.rows, 0, d.rows + d.s)
            rows = take_rows(slots, place, d.rows, window)
            good = (wide_label[b, :, window] == label) & (row_label[...] == label)
            wide[:, window] = jnp.where(good, rows, wide[:, window])
        out_ref[:, b * d.v : (b + 1) * d.v] = wide[:, : d.v]


def per_device(integrals, ladder, pair_energy, virt_energy, pair_irrep, virt_irrep):
    d = Dims()
    d.con = lax.axis_size("con")
    d.sub = lax.axis_size("sub")
    d.rs = lax.axis_size("rep") * d.sub
    d.rows, d.cols = integrals.shape
    d.v = ladder.shape[0]
    d.m = d.cols // d.v
    d.s = pair_irrep.shape[0] * 3 // 16
    tiles = pl.cdiv(d.v, 128)
    d.w = 128 * pl.cdiv(d.v // 4 + 128, 128)
    d.cw = 128 * pl.cdiv(tiles, d.rs)
    d.vp = d.cw * d.rs
    d.pw = max(d.vp, 128 * (tiles - 1) + d.w)
    con_index = lax.axis_index("con")
    rs_index = lax.axis_index(("rep", "sub"))
    f32 = jnp.float32
    i32 = jnp.int32

    labels = jnp.arange(LABELS, dtype=i32)

    def below(values, upto):
        return jnp.sum((values[None, :] < upto[:, None]).astype(i32), axis=1)

    virt_local = lax.dynamic_slice_in_dim(virt_irrep, rs_index * d.cols, d.cols)
    virt_own = lax.dynamic_slice_in_dim(virt_irrep, con_index * d.v, d.v)
    row_label = lax.dynamic_slice_in_dim(pair_irrep, con_index * d.rows, d.rows)[:, None]
    row_start = below(pair_irrep, labels)
    row_count = below(pair_irrep, labels + 1) - row_start
    blocks = virt_local.reshape(d.m, d.v)
    info = jnp.stack(
        [row_start, row_count]
        + [below(blocks[b], labels) for b in range(d.m)]
        + [below(virt_own, labels), below(virt_own, labels + 1)]
    )
    info = jnp.minimum(info, jnp.where(jnp.arange(d.m + 4)[:, None] < 2, 1 << 20, d.v))
    info = info.at[2 : 2 + d.m].min(d.v - 1)
    pad = ((0, 0), (0, d.pw - d.v))
    wide_label = jnp.pad(blocks, pad, constant_values=-1)[:, None, :]
    wide_energy = jnp.pad(virt_energy.reshape(d.m, d.v), pad)[:, None, :]
    col_label = virt_local[None, :]

    limit = pltpu.CompilerParams(vmem_limit_bytes=48 * 1024 * 1024)
    packed = pl.pallas_call(
        functools.partial(pack_kernel, d),
        out_shape=jax.ShapeDtypeStruct((d.m, d.rows, d.w), f32),
        in_specs=[SMEM, VMEM, VMEM, VMEM],
        out_specs=VMEM,
        scratch_shapes=[pltpu.VMEM((d.rows, d.pw), f32)],
        compiler_params=limit,
    )(info, integrals, row_label, pair_energy[:, None])

    line_sems = [pltpu.SemaphoreType.DMA((d.con - 1,))] * 4
    got = pl.pallas_call(
        functools.partial(gather_kernel, d),
        out_shape=jax.ShapeDtypeStruct((d.m, d.con * d.rows + d.s + 8, d.w), f32),
        in_specs=[VMEM],
        out_specs=VMEM,
        scratch_shapes=line_sems,
        compiler_params=pltpu.CompilerParams(
            collective_id=0, has_side_effects=True, vmem_limit_bytes=32 * 1024 * 1024
        ),
    )(packed)

    piece = (d.rs, d.s, d.cw)
    last_block = pl.cdiv(d.v, d.cw) - 1
    ladder_spec = pl.BlockSpec((d.cw, d.cols), lambda i: (jnp.minimum(i, last_block), 0))
    out_spec = pl.BlockSpec((1, d.s, d.cw), lambda i: (i, 0, 0))
    keep = [
        pltpu.VMEM((d.s, d.cols), f32),
        pltpu.VMEM((2 * d.s, d.cols), jnp.bfloat16),
        pltpu.VMEM((1, d.cols), i32),
        pltpu.VMEM((1, d.cols), i32),
    ]
    slot = jax.ShapeDtypeStruct((d.m, d.s, d.pw), f32)
    part, ints, divisor = pl.pallas_call(
        functools.partial(first_kernel, d),
        grid=(d.rs,),
        out_shape=(jax.ShapeDtypeStruct(piece, f32), slot, slot),
        in_specs=[SMEM, VMEM, VMEM, VMEM, VMEM, ladder_spec],
        out_specs=(out_spec, VMEM, VMEM),
        scratch_shapes=keep,
        compiler_params=limit,
    )(info, got, wide_label, wide_energy, col_label, ladder)

    for repeat in range(ITERS):
        if repeat > 0:
            part = pl.pallas_call(
                functools.partial(next_kernel, d),
                grid=(d.rs,),
                out_shape=jax.ShapeDtypeStruct(piece, f32),
                in_specs=[SMEM, VMEM, VMEM, VMEM, VMEM, ladder_spec],
                out_specs=out_spec,
                scratch_shapes=keep,
                compiler_params=limit,
            )(info, summed, ints, divisor, col_label, ladder)
        summed = pl.pallas_call(
            functools.partial(reduce_kernel, d),
            out_shape=jax.ShapeDtypeStruct((d.m,) + piece, f32),
            in_specs=[VMEM],
            out_specs=VMEM,
            scratch_shapes=[
                pltpu.VMEM((d.rs - 1, d.s, d.cw), f32),
                pltpu.VMEM((d.con, d.s, d.cw), f32),
                pltpu.SemaphoreType.DMA((d.rs - 1,)),
                pltpu.SemaphoreType.DMA((d.rs - 1,)),
                pltpu.SemaphoreType.DMA((d.con,)),
                pltpu.SemaphoreType.DMA((d.m, d.rs)),
            ]
            + line_sems,
            compiler_params=pltpu.CompilerParams(
                collective_id=1 + repeat, has_side_effects=True, vmem_limit_bytes=32 * 1024 * 1024
            ),
        )(part)

    return pl.pallas_call(
        functools.partial(final_kernel, d),
        out_shape=jax.ShapeDtypeStruct((d.rows, d.cols), f32),
        in_specs=[SMEM, VMEM, VMEM, VMEM, VMEM, VMEM],
        out_specs=VMEM,
        scratch_shapes=[
            pltpu.VMEM((2 * d.rows + d.s + 8, d.pw), f32),
            pltpu.VMEM((d.rows, d.pw), f32),
        ],
        compiler_params=limit,
    )(info, summed, ints, divisor, wide_label, row_label)


def solution(mesh):
    in_specs = (
        P(("grp", "con"), ("rep", "sub")),
        P(("grp", "con"), ("rep", "sub")),
        P(("grp", "con")),
        P(("grp", "rep", "sub")),
        P("grp"),
        P("grp"),
    )
    out_specs = P(("grp", "con"), ("rep", "sub"))
    return jax.shard_map(
        per_device, mesh=mesh, in_specs=in_specs, out_specs=out_specs, check_vma=False
    )
```

```python
import functools

import jax
import jax.numpy as jnp
from jax import lax
from jax.experimental import pallas as pl
from jax.experimental.pallas import tpu as pltpu
from jax.sharding import PartitionSpec as P

ITERS = 2
LABELS = 8
PARTS = 2
CHUNK = 256
MESH = pl.DeviceIdType.MESH
VMEM = pl.BlockSpec(memory_space=pltpu.VMEM)
SMEM = pl.BlockSpec(memory_space=pltpu.SMEM)


class Dims:
    pass


def take_rows(ref, start, count, *window):
    shift = start % 8
    rows = ref[(*window[:-1], pl.ds(pl.multiple_of(start - shift, 8), count + 8), window[-1])]
    return pltpu.roll(rows, (count + 8 - shift) % (count + 8), 0)[:count]


def pack_kernel(d, tiles, x_ref, label_ref, energy_ref, out_ref, wide):
    for b in range(d.m):
        wide[:, (d.v // 128) * 128 :] = jnp.zeros_like(wide[:, (d.v // 128) * 128 :])
        wide[:, : d.v] = x_ref[:, b * d.v : (b + 1) * d.v]
        value = jnp.zeros((d.rows, d.w), jnp.float32)
        for label in range(LABELS):
            shift = tiles[2 + b, label] % 128
            start = pl.multiple_of(tiles[2 + b, label] - shift, 128)
            window = pltpu.roll(wide[:, pl.ds(start, d.w + 128)], d.w + 128 - shift, 1)
            value = jnp.where(label_ref[...] == label, window[:, : d.w], value)
        lane = lax.broadcasted_iota(jnp.int32, (d.rows, d.w), 1)
        out_ref[b] = jnp.where(lane == d.w - 1, energy_ref[...], value)


def line_copies(z, n, view, up_send, up_recv, down_send, down_recv):
    def at(t):
        up_block = jnp.maximum(z - t, 0)
        down_block = jnp.minimum(z + t, n - 1)
        up = pltpu.make_async_remote_copy(
            src_ref=view(up_block),
            dst_ref=view(up_block),
            send_sem=up_send.at[t],
            recv_sem=up_recv.at[t],
            device_id={"con": jnp.minimum(z + 1, n - 1)},
            device_id_type=MESH,
        )
        down = pltpu.make_async_remote_copy(
            src_ref=view(down_block),
            dst_ref=view(down_block),
            send_sem=down_send.at[t],
            recv_sem=down_recv.at[t],
            device_id={"con": jnp.maximum(z - 1, 0)},
            device_id_type=MESH,
        )
        return up, down, (z >= t) & (z < n - 1), (z + t <= n - 1) & (z > 0)

    return at


def line_gather(z, n, view, sems, ready, arrived):
    at = [
        line_copies(z, n, functools.partial(view, h), *[sem.at[h] for sem in sems])
        for h in range(PARTS)
    ]

    def send(h, t):
        up, down, can_up, can_down = at[h](t)
        pl.when(can_up)(up.start)
        pl.when(can_down)(down.start)

    for h in range(PARTS):
        ready(h)
        send(h, 0)
        arrived(h, z)
    for t in range(n - 1):
        for h in range(PARTS):
            up, down, _, _ = at[h](t)
            pl.when(z - 1 - t >= 0)(up.wait_recv)
            pl.when(z + 1 + t <= n - 1)(down.wait_recv)
            if t + 1 < n - 1:
                send(h, t + 1)

            @pl.when(z - 1 - t >= 0)
            def _():
                arrived(h, z - 1 - t)

            @pl.when(z + 1 + t <= n - 1)
            def _():
                arrived(h, z + 1 + t)

    for t in range(n - 1):
        for h in range(PARTS):
            up, down, can_up, can_down = at[h](t)
            pl.when(can_up)(up.wait_send)
            pl.when(can_down)(down.wait_send)


def greet(z, n, others):
    barrier = pltpu.get_barrier_semaphore()
    for other in others:
        pl.semaphore_signal(barrier, inc=1, device_id=other, device_id_type=MESH)

    @pl.when(z > 0)
    def _():
        pl.semaphore_signal(barrier, inc=1, device_id={"con": z - 1}, device_id_type=MESH)

    @pl.when(z < n - 1)
    def _():
        pl.semaphore_signal(barrier, inc=1, device_id={"con": z + 1}, device_id_type=MESH)

    near = (z > 0).astype(jnp.int32) + (z < n - 1).astype(jnp.int32)
    pl.semaphore_wait(barrier, near + len(others))


def gather_kernel(d, x_ref, out_ref, *sems):
    z = lax.axis_index("con")
    greet(z, d.con, [])

    rows = d.rows // PARTS

    def view(h, block):
        return out_ref.at[:, pl.ds(pl.multiple_of(block * d.rows + h * rows, 8), rows), :]

    out_ref[:, pl.ds(pl.multiple_of(z * d.rows, 8), d.rows), :] = x_ref[...]
    line_gather(z, d.con, view, sems, lambda h: None, lambda h, block: None)


def reduce_kernel(d, x_ref, out_ref, landed, whole, s_send, s_recv, x_send, x_recv, *sems):
    z = lax.axis_index("con")
    j = lax.axis_index("rep") * d.sub + lax.axis_index("sub")

    def device(q):
        return {"rep": q // d.sub, "sub": q % d.sub}

    greet(z, d.con, [device((j + k) % d.rs) for k in range(1, d.rs)])
    rows = d.s // PARTS
    part = [pl.ds(h * rows, rows) for h in range(PARTS)]
    copies = []
    for h in range(PARTS):
        for k in range(1, d.rs):
            q = (j + k) % d.rs
            copy = pltpu.make_async_remote_copy(
                src_ref=x_ref.at[q, part[h]],
                dst_ref=landed.at[k - 1, part[h]],
                send_sem=s_send.at[h, k - 1],
                recv_sem=s_recv.at[h, k - 1],
                device_id=device(q),
                device_id_type=MESH,
            )
            copy.start()
            copies.append(copy)

    def ready(h):
        total = x_ref[j, part[h]]
        for k in range(1, d.rs):
            copies[h * (d.rs - 1) + k - 1].wait_recv()
            total = total + landed[k - 1, part[h]]
        whole[z, part[h]] = total

    def to_owner(h, block):
        owner = block // d.m
        return owner, pltpu.make_async_remote_copy(
            src_ref=whole.at[block, part[h]],
            dst_ref=out_ref.at[block % d.m, j, part[h]],
            send_sem=x_send.at[h, block],
            recv_sem=x_recv.at[h, block % d.m, j],
            device_id=device(owner),
            device_id_type=MESH,
        )

    def arrived(h, block):
        owner, copy = to_owner(h, block)
        pl.when(owner != j)(copy.start)

        @pl.when(owner == j)
        def _():
            out_ref[block % d.m, j, part[h]] = whole[block, part[h]]

    line_gather(z, d.con, lambda h, block: whole.at[block, part[h]], sems, ready, arrived)
    for h in range(PARTS):
        for block in range(d.con):
            owner, copy = to_owner(h, block)
            pl.when(owner != j)(copy.wait_send)
        for b in range(d.m):
            for k in range(1, d.rs):
                q = (j + k) % d.rs
                pltpu.make_async_remote_copy(
                    src_ref=whole.at[0, part[h]],
                    dst_ref=out_ref.at[b, q, part[h]],
                    send_sem=x_send.at[h, 0],
                    recv_sem=x_recv.at[h, b, q],
                    device_id=device(q),
                    device_id_type=MESH,
                ).wait_recv()
    for copy in copies:
        copy.wait_send()


def product(d, spans, ladder_ref, out_ref, high_low, low, high, acc):
    step = pl.program_id(0)
    dims = (((1,), (1,)), ((), ()))
    acc[...] = jnp.zeros_like(acc)
    for half in range(2):
        mine = d.chunks + step * 2 + half
        here = pl.ds(half * d.half, d.half)
        for chunk in range(d.chunks):
            cut = slice(chunk * CHUNK, min((chunk + 1) * CHUNK, d.cols))

            @pl.when((spans[0, mine] <= spans[1, chunk]) & (spans[0, chunk] <= spans[1, mine]))
            def _():
                row = lax.broadcasted_iota(jnp.int32, (d.half, cut.stop - cut.start), 0)
                row = row + (step * d.cw + half * d.half)
                keep = (row >= low[:, cut]) & (row < high[:, cut])
                value = jnp.where(keep, ladder_ref[here, cut], 0.0)
                value_high = value.astype(jnp.bfloat16)
                value_low = (value - value_high.astype(jnp.float32)).astype(jnp.bfloat16)
                first = lax.dot_general(
                    value_high, high_low[:, cut], dims, preferred_element_type=jnp.float32
                )
                second = lax.dot_general(
                    value_low, high_low[: d.s, cut], dims, preferred_element_type=jnp.float32
                )
                acc[here, :] += first[:, : d.s] + first[:, d.s :] + second

    out_ref[0] = jnp.transpose(acc[...])


def prepare(d, info, label_ref, amp, high_low, low, high):
    value = amp[...]
    value_high = value.astype(jnp.bfloat16)
    high_low[: d.s, :] = value_high
    high_low[d.s :, :] = (value - value_high.astype(jnp.float32)).astype(jnp.bfloat16)
    first = jnp.zeros((1, d.cols), jnp.int32)
    last = jnp.zeros((1, d.cols), jnp.int32)
    for label in range(LABELS):
        here = label_ref[...] == label
        first = jnp.where(here, info[2 + d.m, label], first)
        last = jnp.where(here, info[3 + d.m, label], last)
    low[...] = first
    high[...] = last


def first_kernel(
    d, info, spans, got_ref, wide_label, wide_energy, label_ref, ladder_ref,
    out_ref, ints_ref, div_ref, amp, high_low, low, high, acc,
):
    @pl.when(pl.program_id(0) == 0)
    def _():
        ints_ref[...] = jnp.zeros_like(ints_ref)
        div_ref[...] = jnp.ones_like(div_ref)
        slot = lax.broadcasted_iota(jnp.int32, (d.s, d.w + 128), 0)
        for b in range(d.m):
            for label in range(LABELS):
                shift = info[2 + b, label] % 128
                start = pl.multiple_of(info[2 + b, label] - shift, 128)
                rows = take_rows(got_ref, info[0, label], d.s, b, slice(None))
                energy = rows[:, d.w - 1 : d.w]
                rows = jnp.concatenate([rows, jnp.zeros((d.s, 128), jnp.float32)], axis=1)
                rows = pltpu.roll(rows, shift, 1)
                window = pl.ds(start, d.w + 128)
                good = (wide_label[b, :, window] == label) & (slot < info[1, label])
                divisor = wide_energy[b, :, window] - energy
                ints_ref[b, :, window] = jnp.where(good, rows, ints_ref[b, :, window])
                div_ref[b, :, window] = jnp.where(good, divisor, div_ref[b, :, window])
            amp[:, b * d.v : (b + 1) * d.v] = ints_ref[b, :, : d.v] / div_ref[b, :, : d.v]
        prepare(d, info, label_ref, amp, high_low, low, high)

    product(d, spans, ladder_ref, out_ref, high_low, low, high, acc)


def update(d, b, sum_ref, ints_ref, div_ref):
    term = jnp.concatenate([sum_ref[b, q] for q in range(d.rs)], axis=1)
    return (ints_ref[b, :, : d.vp] + term) / div_ref[b, :, : d.vp]


def next_kernel(
    d, info, spans, sum_ref, ints_ref, div_ref, label_ref, ladder_ref,
    out_ref, amp, high_low, low, high, acc,
):
    @pl.when(pl.program_id(0) == 0)
    def _():
        for b in range(d.m):
            amp[:, b * d.v : (b + 1) * d.v] = update(d, b, sum_ref, ints_ref, div_ref)[:, : d.v]
        prepare(d, info, label_ref, amp, high_low, low, high)

    product(d, spans, ladder_ref, out_ref, high_low, low, high, acc)


def final_kernel(d, info, sum_ref, ints_ref, div_ref, wide_label, row_label, out_ref, slots, wide):
    base = lax.axis_index("con") * d.rows
    for b in range(d.m):
        slots[...] = jnp.zeros_like(slots)
        slots[d.rows : d.rows + d.s, : d.vp] = update(d, b, sum_ref, ints_ref, div_ref)
        wide[...] = jnp.zeros_like(wide)
        for label in range(LABELS):
            start = pl.multiple_of(info[2 + b, label] // 128 * 128, 128)
            window = pl.ds(start, d.w + 128)
            place = jnp.clip(base - info[0, label] + d.rows, 0, d.rows + d.s)
            rows = take_rows(slots, place, d.rows, window)
            good = (wide_label[b, :, window] == label) & (row_label[...] == label)
            wide[:, window] = jnp.where(good, rows, wide[:, window])
        out_ref[:, b * d.v : (b + 1) * d.v] = wide[:, : d.v]


def per_device(integrals, ladder, pair_energy, virt_energy, pair_irrep, virt_irrep):
    d = Dims()
    d.con = lax.axis_size("con")
    d.sub = lax.axis_size("sub")
    d.rs = lax.axis_size("rep") * d.sub
    d.rows, d.cols = integrals.shape
    d.v = ladder.shape[0]
    d.m = d.cols // d.v
    d.s = pair_irrep.shape[0] * 3 // 16
    tiles = pl.cdiv(d.v, 128)
    d.w = 128 * pl.cdiv(d.v // 4 + 1, 128)
    d.cw = 128 * pl.cdiv(tiles, d.rs)
    d.vp = d.cw * d.rs
    d.pw = max(d.vp, 128 * tiles + d.w)
    con_index = lax.axis_index("con")
    rs_index = lax.axis_index(("rep", "sub"))
    f32 = jnp.float32
    i32 = jnp.int32

    labels = jnp.arange(LABELS, dtype=i32)

    def below(values, upto):
        return jnp.sum((values[None, :] < upto[:, None]).astype(i32), axis=1)

    virt_local = lax.dynamic_slice_in_dim(virt_irrep, rs_index * d.cols, d.cols)
    virt_own = lax.dynamic_slice_in_dim(virt_irrep, con_index * d.v, d.v)
    row_label = lax.dynamic_slice_in_dim(pair_irrep, con_index * d.rows, d.rows)[:, None]
    row_start = below(pair_irrep, labels)
    row_count = below(pair_irrep, labels + 1) - row_start
    blocks = virt_local.reshape(d.m, d.v)
    info = jnp.stack(
        [row_start, row_count]
        + [below(blocks[b], labels) for b in range(d.m)]
        + [below(virt_own, labels), below(virt_own, labels + 1)]
    )
    info = jnp.minimum(info, jnp.where(jnp.arange(d.m + 4)[:, None] < 2, 1 << 20, d.v))
    info = info.at[2 : 2 + d.m].min(d.v - 1)
    d.half = d.cw // 2
    d.chunks = pl.cdiv(d.cols, CHUNK)

    def cuts(values, count, size):
        return jnp.pad(values, (0, count * size - values.shape[0]), mode="edge").reshape(count, size)

    by_chunk = cuts(virt_local, d.chunks, CHUNK)
    by_half = cuts(virt_own, 2 * d.rs, d.half)
    spans = jnp.stack(
        [
            jnp.concatenate([by_chunk.min(axis=1), by_half.min(axis=1)]),
            jnp.concatenate([by_chunk.max(axis=1), by_half.max(axis=1)]),
        ]
    )
    pad = ((0, 0), (0, d.pw - d.v))
    wide_label = jnp.pad(blocks, pad, constant_values=-1)[:, None, :]
    wide_energy = jnp.pad(virt_energy.reshape(d.m, d.v), pad)[:, None, :]
    col_label = virt_local[None, :]

    limit = pltpu.CompilerParams(vmem_limit_bytes=48 * 1024 * 1024)
    packed = pl.pallas_call(
        functools.partial(pack_kernel, d),
        out_shape=jax.ShapeDtypeStruct((d.m, d.rows, d.w), f32),
        in_specs=[SMEM, VMEM, VMEM, VMEM],
        out_specs=VMEM,
        scratch_shapes=[pltpu.VMEM((d.rows, d.pw), f32)],
        compiler_params=limit,
    )(info, integrals, row_label, pair_energy[:, None])

    line_sems = [pltpu.SemaphoreType.DMA((PARTS, d.con - 1))] * 4
    got = pl.pallas_call(
        functools.partial(gather_kernel, d),
        out_shape=jax.ShapeDtypeStruct((d.m, d.con * d.rows + d.s + 8, d.w), f32),
        in_specs=[VMEM],
        out_specs=VMEM,
        scratch_shapes=line_sems,
        compiler_params=pltpu.CompilerParams(
            collective_id=0, has_side_effects=True, vmem_limit_bytes=32 * 1024 * 1024
        ),
    )(packed)

    piece = (d.rs, d.s, d.cw)
    last_block = pl.cdiv(d.v, d.cw) - 1
    ladder_spec = pl.BlockSpec((d.cw, d.cols), lambda i: (jnp.minimum(i, last_block), 0))
    out_spec = pl.BlockSpec((1, d.s, d.cw), lambda i: (i, 0, 0))
    keep = [
        pltpu.VMEM((d.s, d.cols), f32),
        pltpu.VMEM((2 * d.s, d.cols), jnp.bfloat16),
        pltpu.VMEM((1, d.cols), i32),
        pltpu.VMEM((1, d.cols), i32),
        pltpu.VMEM((d.cw, d.s), f32),
    ]
    slot = jax.ShapeDtypeStruct((d.m, d.s, d.pw), f32)
    part, ints, divisor = pl.pallas_call(
        functools.partial(first_kernel, d),
        grid=(d.rs,),
        out_shape=(jax.ShapeDtypeStruct(piece, f32), slot, slot),
        in_specs=[SMEM, SMEM, VMEM, VMEM, VMEM, VMEM, ladder_spec],
        out_specs=(out_spec, VMEM, VMEM),
        scratch_shapes=keep,
        compiler_params=limit,
    )(info, spans, got, wide_label, wide_energy, col_label, ladder)

    for repeat in range(ITERS):
        if repeat > 0:
            part = pl.pallas_call(
                functools.partial(next_kernel, d),
                grid=(d.rs,),
                out_shape=jax.ShapeDtypeStruct(piece, f32),
                in_specs=[SMEM, SMEM, VMEM, VMEM, VMEM, VMEM, ladder_spec],
                out_specs=out_spec,
                scratch_shapes=keep,
                compiler_params=limit,
            )(info, spans, summed, ints, divisor, col_label, ladder)
        summed = pl.pallas_call(
            functools.partial(reduce_kernel, d),
            out_shape=jax.ShapeDtypeStruct((d.m,) + piece, f32),
            in_specs=[VMEM],
            out_specs=VMEM,
            scratch_shapes=[
                pltpu.VMEM((d.rs - 1, d.s, d.cw), f32),
                pltpu.VMEM((d.con, d.s, d.cw), f32),
                pltpu.SemaphoreType.DMA((PARTS, d.rs - 1)),
                pltpu.SemaphoreType.DMA((PARTS, d.rs - 1)),
                pltpu.SemaphoreType.DMA((PARTS, d.con)),
                pltpu.SemaphoreType.DMA((PARTS, d.m, d.rs)),
            ]
            + line_sems,
            compiler_params=pltpu.CompilerParams(
                collective_id=1 + repeat, has_side_effects=True, vmem_limit_bytes=32 * 1024 * 1024
            ),
        )(part)

    return pl.pallas_call(
        functools.partial(final_kernel, d),
        out_shape=jax.ShapeDtypeStruct((d.rows, d.cols), f32),
        in_specs=[SMEM, VMEM, VMEM, VMEM, VMEM, VMEM],
        out_specs=VMEM,
        scratch_shapes=[
            pltpu.VMEM((2 * d.rows + d.s + 8, d.pw), f32),
            pltpu.VMEM((d.rows, d.pw), f32),
        ],
        compiler_params=limit,
    )(info, summed, ints, divisor, wide_label, row_label)


def solution(mesh):
    in_specs = (
        P(("grp", "con"), ("rep", "sub")),
        P(("grp", "con"), ("rep", "sub")),
        P(("grp", "con")),
        P(("grp", "rep", "sub")),
        P("grp"),
        P("grp"),
    )
    out_specs = P(("grp", "con"), ("rep", "sub"))
    return jax.shard_map(
        per_device, mesh=mesh, in_specs=in_specs, out_specs=out_specs, check_vma=False
    )
```

```python
import functools

import jax
import jax.numpy as jnp
from jax import lax
from jax.experimental import pallas as pl
from jax.experimental.pallas import tpu as pltpu
from jax.sharding import PartitionSpec as P

ITERS = 2
LABELS = 8
PARTS = 2
CHUNK = 256
STREAMS = 4
MESH = pl.DeviceIdType.MESH
VMEM = pl.BlockSpec(memory_space=pltpu.VMEM)
SMEM = pl.BlockSpec(memory_space=pltpu.SMEM)


class Dims:
    pass


def take_rows(ref, start, count, *window):
    shift = start % 8
    rows = ref[(*window[:-1], pl.ds(pl.multiple_of(start - shift, 8), count + 8), window[-1])]
    return pltpu.roll(rows, (count + 8 - shift) % (count + 8), 0)[:count]


def pack_kernel(d, tiles, x_ref, label_ref, energy_ref, out_ref, wide):
    for b in range(d.m):
        wide[:, (d.v // 128) * 128 :] = jnp.zeros_like(wide[:, (d.v // 128) * 128 :])
        wide[:, : d.v] = x_ref[:, b * d.v : (b + 1) * d.v]
        value = jnp.zeros((d.rows, d.w), jnp.float32)
        for label in range(LABELS):
            shift = tiles[2 + b, label] % 128
            start = pl.multiple_of(tiles[2 + b, label] - shift, 128)
            window = pltpu.roll(wide[:, pl.ds(start, d.w + 128)], d.w + 128 - shift, 1)
            value = jnp.where(label_ref[...] == label, window[:, : d.w], value)
        lane = lax.broadcasted_iota(jnp.int32, (d.rows, d.w), 1)
        out_ref[b] = jnp.where(lane == d.w - 1, energy_ref[...], value)


def line_copies(z, n, view, up_send, up_recv, down_send, down_recv):
    def at(t):
        up_block = jnp.maximum(z - t, 0)
        down_block = jnp.minimum(z + t, n - 1)
        up = pltpu.make_async_remote_copy(
            src_ref=view(up_block),
            dst_ref=view(up_block),
            send_sem=up_send.at[t],
            recv_sem=up_recv.at[t],
            device_id={"con": jnp.minimum(z + 1, n - 1)},
            device_id_type=MESH,
        )
        down = pltpu.make_async_remote_copy(
            src_ref=view(down_block),
            dst_ref=view(down_block),
            send_sem=down_send.at[t],
            recv_sem=down_recv.at[t],
            device_id={"con": jnp.maximum(z - 1, 0)},
            device_id_type=MESH,
        )
        return up, down, (z >= t) & (z < n - 1), (z + t <= n - 1) & (z > 0)

    return at


def line_gather(z, n, view, sems, ready, arrived):
    at = [
        line_copies(z, n, functools.partial(view, h), *[sem.at[h] for sem in sems])
        for h in range(PARTS)
    ]

    def send(h, t):
        up, down, can_up, can_down = at[h](t)
        pl.when(can_up)(up.start)
        pl.when(can_down)(down.start)

    for h in range(PARTS):
        ready(h)
        send(h, 0)
        arrived(h, z)
    for t in range(n - 1):
        for h in range(PARTS):
            up, down, _, _ = at[h](t)
            pl.when(z - 1 - t >= 0)(up.wait_recv)
            pl.when(z + 1 + t <= n - 1)(down.wait_recv)
            if t + 1 < n - 1:
                send(h, t + 1)

            @pl.when(z - 1 - t >= 0)
            def _():
                arrived(h, z - 1 - t)

            @pl.when(z + 1 + t <= n - 1)
            def _():
                arrived(h, z + 1 + t)

    for t in range(n - 1):
        for h in range(PARTS):
            up, down, can_up, can_down = at[h](t)
            pl.when(can_up)(up.wait_send)
            pl.when(can_down)(down.wait_send)


def greet(z, n, others):
    barrier = pltpu.get_barrier_semaphore()
    for other in others:
        pl.semaphore_signal(barrier, inc=1, device_id=other, device_id_type=MESH)

    @pl.when(z > 0)
    def _():
        pl.semaphore_signal(barrier, inc=1, device_id={"con": z - 1}, device_id_type=MESH)

    @pl.when(z < n - 1)
    def _():
        pl.semaphore_signal(barrier, inc=1, device_id={"con": z + 1}, device_id_type=MESH)

    near = (z > 0).astype(jnp.int32) + (z < n - 1).astype(jnp.int32)
    pl.semaphore_wait(barrier, near + len(others))


def gather_kernel(d, x_ref, out_ref, *sems):
    z = lax.axis_index("con")
    greet(z, d.con, [])

    rows = d.rows // PARTS

    def view(h, block):
        return out_ref.at[:, pl.ds(pl.multiple_of(block * d.rows + h * rows, 8), rows), :]

    out_ref[:, pl.ds(pl.multiple_of(z * d.rows, 8), d.rows), :] = x_ref[...]
    line_gather(z, d.con, view, sems, lambda h: None, lambda h, block: None)


def reduce_kernel(d, x_ref, out_ref, landed, whole, s_send, s_recv, x_send, x_recv, *sems):
    z = lax.axis_index("con")
    j = lax.axis_index("rep") * d.sub + lax.axis_index("sub")

    def device(q):
        return {"rep": q // d.sub, "sub": q % d.sub}

    greet(z, d.con, [device((j + k) % d.rs) for k in range(1, d.rs)])
    rows = d.s // PARTS
    part = [pl.ds(h * rows, rows) for h in range(PARTS)]
    copies = []
    for h in range(PARTS):
        for k in range(1, d.rs):
            q = (j + k) % d.rs
            copy = pltpu.make_async_remote_copy(
                src_ref=x_ref.at[q, part[h]],
                dst_ref=landed.at[k - 1, part[h]],
                send_sem=s_send.at[h, k - 1],
                recv_sem=s_recv.at[h, k - 1],
                device_id=device(q),
                device_id_type=MESH,
            )
            copy.start()
            copies.append(copy)

    def ready(h):
        total = x_ref[j, part[h]]
        for k in range(1, d.rs):
            copies[h * (d.rs - 1) + k - 1].wait_recv()
            total = total + landed[k - 1, part[h]]
        whole[z, part[h]] = total

    def to_owner(h, block):
        owner = block // d.m
        return owner, pltpu.make_async_remote_copy(
            src_ref=whole.at[block, part[h]],
            dst_ref=out_ref.at[block % d.m, j, part[h]],
            send_sem=x_send.at[h, block],
            recv_sem=x_recv.at[h, block % d.m, j],
            device_id=device(owner),
            device_id_type=MESH,
        )

    def arrived(h, block):
        owner, copy = to_owner(h, block)
        pl.when(owner != j)(copy.start)

        @pl.when(owner == j)
        def _():
            out_ref[block % d.m, j, part[h]] = whole[block, part[h]]

    line_gather(z, d.con, lambda h, block: whole.at[block, part[h]], sems, ready, arrived)
    for h in range(PARTS):
        for block in range(d.con):
            owner, copy = to_owner(h, block)
            pl.when(owner != j)(copy.wait_send)
        for b in range(d.m):
            for k in range(1, d.rs):
                q = (j + k) % d.rs
                pltpu.make_async_remote_copy(
                    src_ref=whole.at[0, part[h]],
                    dst_ref=out_ref.at[b, q, part[h]],
                    send_sem=x_send.at[h, 0],
                    recv_sem=x_recv.at[h, b, q],
                    device_id=device(q),
                    device_id_type=MESH,
                ).wait_recv()
    for copy in copies:
        copy.wait_send()


def product(d, spans, ladder_refs, out_ref, high_low, low, high, acc):
    step = pl.program_id(0)
    dims = (((1,), (1,)), ((), ()))
    acc[...] = jnp.zeros_like(acc)
    for half in range(STREAMS):
        mine = d.chunks + step * STREAMS + half
        here = pl.ds(half * d.half, d.half)
        for chunk in range(d.chunks):
            cut = slice(chunk * CHUNK, min((chunk + 1) * CHUNK, d.cols))

            @pl.when((spans[0, mine] <= spans[1, chunk]) & (spans[0, chunk] <= spans[1, mine]))
            def _():
                row = lax.broadcasted_iota(jnp.int32, (d.half, cut.stop - cut.start), 0)
                row = row + (step * d.cw + half * d.half)
                keep = (row >= low[:, cut]) & (row < high[:, cut])
                value = jnp.where(keep, ladder_refs[half][:, cut], 0.0)
                value_high = value.astype(jnp.bfloat16)
                value_low = (value - value_high.astype(jnp.float32)).astype(jnp.bfloat16)
                first = lax.dot_general(
                    value_high, high_low[:, cut], dims, preferred_element_type=jnp.float32
                )
                second = lax.dot_general(
                    value_low, high_low[: d.s, cut], dims, preferred_element_type=jnp.float32
                )
                acc[here, :] += first[:, : d.s] + first[:, d.s :] + second

    out_ref[0] = jnp.transpose(acc[...])


def prepare(d, info, label_ref, amp, high_low, low, high):
    value = amp[...]
    value_high = value.astype(jnp.bfloat16)
    high_low[: d.s, :] = value_high
    high_low[d.s :, :] = (value - value_high.astype(jnp.float32)).astype(jnp.bfloat16)
    first = jnp.zeros((1, d.cols), jnp.int32)
    last = jnp.zeros((1, d.cols), jnp.int32)
    for label in range(LABELS):
        here = label_ref[...] == label
        first = jnp.where(here, info[2 + d.m, label], first)
        last = jnp.where(here, info[3 + d.m, label], last)
    low[...] = first
    high[...] = last


def first_kernel(
    d, info, spans, got_ref, wide_label, wide_energy, label_ref, l0, l1, l2, l3,
    out_ref, ints_ref, div_ref, amp, high_low, low, high, acc,
):
    @pl.when(pl.program_id(0) == 0)
    def _():
        ints_ref[...] = jnp.zeros_like(ints_ref)
        div_ref[...] = jnp.ones_like(div_ref)
        slot = lax.broadcasted_iota(jnp.int32, (d.s, d.w + 128), 0)
        for b in range(d.m):
            for label in range(LABELS):
                shift = info[2 + b, label] % 128
                start = pl.multiple_of(info[2 + b, label] - shift, 128)
                rows = take_rows(got_ref, info[0, label], d.s, b, slice(None))
                energy = rows[:, d.w - 1 : d.w]
                rows = jnp.concatenate([rows, jnp.zeros((d.s, 128), jnp.float32)], axis=1)
                rows = pltpu.roll(rows, shift, 1)
                window = pl.ds(start, d.w + 128)
                good = (wide_label[b, :, window] == label) & (slot < info[1, label])
                divisor = wide_energy[b, :, window] - energy
                ints_ref[b, :, window] = jnp.where(good, rows, ints_ref[b, :, window])
                div_ref[b, :, window] = jnp.where(good, divisor, div_ref[b, :, window])
            amp[:, b * d.v : (b + 1) * d.v] = ints_ref[b, :, : d.v] / div_ref[b, :, : d.v]
        prepare(d, info, label_ref, amp, high_low, low, high)

    product(d, spans, (l0, l1, l2, l3), out_ref, high_low, low, high, acc)


def update(d, b, sum_ref, ints_ref, div_ref):
    term = jnp.concatenate([sum_ref[b, q] for q in range(d.rs)], axis=1)
    return (ints_ref[b, :, : d.vp] + term) / div_ref[b, :, : d.vp]


def next_kernel(
    d, info, spans, sum_ref, ints_ref, div_ref, label_ref, l0, l1, l2, l3,
    out_ref, amp, high_low, low, high, acc,
):
    @pl.when(pl.program_id(0) == 0)
    def _():
        for b in range(d.m):
            amp[:, b * d.v : (b + 1) * d.v] = update(d, b, sum_ref, ints_ref, div_ref)[:, : d.v]
        prepare(d, info, label_ref, amp, high_low, low, high)

    product(d, spans, (l0, l1, l2, l3), out_ref, high_low, low, high, acc)


def final_kernel(d, info, sum_ref, ints_ref, div_ref, wide_label, row_label, out_ref, slots, wide):
    base = lax.axis_index("con") * d.rows
    for b in range(d.m):
        slots[...] = jnp.zeros_like(slots)
        slots[d.rows : d.rows + d.s, : d.vp] = update(d, b, sum_ref, ints_ref, div_ref)
        wide[...] = jnp.zeros_like(wide)
        for label in range(LABELS):
            start = pl.multiple_of(info[2 + b, label] // 128 * 128, 128)
            window = pl.ds(start, d.w + 128)
            place = jnp.clip(base - info[0, label] + d.rows, 0, d.rows + d.s)
            rows = take_rows(slots, place, d.rows, window)
            good = (wide_label[b, :, window] == label) & (row_label[...] == label)
            wide[:, window] = jnp.where(good, rows, wide[:, window])
        out_ref[:, b * d.v : (b + 1) * d.v] = wide[:, : d.v]


def per_device(integrals, ladder, pair_energy, virt_energy, pair_irrep, virt_irrep):
    d = Dims()
    d.con = lax.axis_size("con")
    d.sub = lax.axis_size("sub")
    d.rs = lax.axis_size("rep") * d.sub
    d.rows, d.cols = integrals.shape
    d.v = ladder.shape[0]
    d.m = d.cols // d.v
    d.s = pair_irrep.shape[0] * 3 // 16
    tiles = pl.cdiv(d.v, 128)
    d.w = 128 * pl.cdiv(d.v // 4 + 1, 128)
    d.cw = 128 * pl.cdiv(tiles, d.rs)
    d.vp = d.cw * d.rs
    d.pw = max(d.vp, 128 * tiles + d.w)
    con_index = lax.axis_index("con")
    rs_index = lax.axis_index(("rep", "sub"))
    f32 = jnp.float32
    i32 = jnp.int32

    labels = jnp.arange(LABELS, dtype=i32)

    def below(values, upto):
        return jnp.sum((values[None, :] < upto[:, None]).astype(i32), axis=1)

    virt_local = lax.dynamic_slice_in_dim(virt_irrep, rs_index * d.cols, d.cols)
    virt_own = lax.dynamic_slice_in_dim(virt_irrep, con_index * d.v, d.v)
    row_label = lax.dynamic_slice_in_dim(pair_irrep, con_index * d.rows, d.rows)[:, None]
    row_start = below(pair_irrep, labels)
    row_count = below(pair_irrep, labels + 1) - row_start
    blocks = virt_local.reshape(d.m, d.v)
    info = jnp.stack(
        [row_start, row_count]
        + [below(blocks[b], labels) for b in range(d.m)]
        + [below(virt_own, labels), below(virt_own, labels + 1)]
    )
    info = jnp.minimum(info, jnp.where(jnp.arange(d.m + 4)[:, None] < 2, 1 << 20, d.v))
    info = info.at[2 : 2 + d.m].min(d.v - 1)
    d.half = d.cw // STREAMS
    d.chunks = pl.cdiv(d.cols, CHUNK)

    def cuts(values, count, size):
        return jnp.pad(values, (0, count * size - values.shape[0]), mode="edge").reshape(count, size)

    by_chunk = cuts(virt_local, d.chunks, CHUNK)
    by_half = cuts(virt_own, STREAMS * d.rs, d.half)
    spans = jnp.stack(
        [
            jnp.concatenate([by_chunk.min(axis=1), by_half.min(axis=1)]),
            jnp.concatenate([by_chunk.max(axis=1), by_half.max(axis=1)]),
        ]
    )
    pad = ((0, 0), (0, d.pw - d.v))
    wide_label = jnp.pad(blocks, pad, constant_values=-1)[:, None, :]
    wide_energy = jnp.pad(virt_energy.reshape(d.m, d.v), pad)[:, None, :]
    col_label = virt_local[None, :]

    limit = pltpu.CompilerParams(vmem_limit_bytes=48 * 1024 * 1024)
    packed = pl.pallas_call(
        functools.partial(pack_kernel, d),
        out_shape=jax.ShapeDtypeStruct((d.m, d.rows, d.w), f32),
        in_specs=[SMEM, VMEM, VMEM, VMEM],
        out_specs=VMEM,
        scratch_shapes=[pltpu.VMEM((d.rows, d.pw), f32)],
        compiler_params=limit,
    )(info, integrals, row_label, pair_energy[:, None])

    line_sems = [pltpu.SemaphoreType.DMA((PARTS, d.con - 1))] * 4
    got = pl.pallas_call(
        functools.partial(gather_kernel, d),
        out_shape=jax.ShapeDtypeStruct((d.m, d.con * d.rows + d.s + 8, d.w), f32),
        in_specs=[VMEM],
        out_specs=VMEM,
        scratch_shapes=line_sems,
        compiler_params=pltpu.CompilerParams(
            collective_id=0, has_side_effects=True, vmem_limit_bytes=32 * 1024 * 1024
        ),
    )(packed)

    piece = (d.rs, d.s, d.cw)
    last_block = pl.cdiv(d.v, d.half) - 1

    def ladder_spec(k):
        return pl.BlockSpec(
            (d.half, d.cols), lambda i: (jnp.minimum(i * STREAMS + k, last_block), 0)
        )

    ladder_specs = [ladder_spec(k) for k in range(STREAMS)]
    out_spec = pl.BlockSpec((1, d.s, d.cw), lambda i: (i, 0, 0))
    keep = [
        pltpu.VMEM((d.s, d.cols), f32),
        pltpu.VMEM((2 * d.s, d.cols), jnp.bfloat16),
        pltpu.VMEM((1, d.cols), i32),
        pltpu.VMEM((1, d.cols), i32),
        pltpu.VMEM((d.cw, d.s), f32),
    ]
    slot = jax.ShapeDtypeStruct((d.m, d.s, d.pw), f32)
    part, ints, divisor = pl.pallas_call(
        functools.partial(first_kernel, d),
        grid=(d.rs,),
        out_shape=(jax.ShapeDtypeStruct(piece, f32), slot, slot),
        in_specs=[SMEM, SMEM, VMEM, VMEM, VMEM, VMEM, *ladder_specs],
        out_specs=(out_spec, VMEM, VMEM),
        scratch_shapes=keep,
        compiler_params=limit,
    )(info, spans, got, wide_label, wide_energy, col_label, *[ladder] * STREAMS)

    for repeat in range(ITERS):
        if repeat > 0:
            part = pl.pallas_call(
                functools.partial(next_kernel, d),
                grid=(d.rs,),
                out_shape=jax.ShapeDtypeStruct(piece, f32),
                in_specs=[SMEM, SMEM, VMEM, VMEM, VMEM, VMEM, *ladder_specs],
                out_specs=out_spec,
                scratch_shapes=keep,
                compiler_params=limit,
            )(info, spans, summed, ints, divisor, col_label, *[ladder] * STREAMS)
        summed = pl.pallas_call(
            functools.partial(reduce_kernel, d),
            out_shape=jax.ShapeDtypeStruct((d.m,) + piece, f32),
            in_specs=[VMEM],
            out_specs=VMEM,
            scratch_shapes=[
                pltpu.VMEM((d.rs - 1, d.s, d.cw), f32),
                pltpu.VMEM((d.con, d.s, d.cw), f32),
                pltpu.SemaphoreType.DMA((PARTS, d.rs - 1)),
                pltpu.SemaphoreType.DMA((PARTS, d.rs - 1)),
                pltpu.SemaphoreType.DMA((PARTS, d.con)),
                pltpu.SemaphoreType.DMA((PARTS, d.m, d.rs)),
            ]
            + line_sems,
            compiler_params=pltpu.CompilerParams(
                collective_id=1 + repeat, has_side_effects=True, vmem_limit_bytes=32 * 1024 * 1024
            ),
        )(part)

    return pl.pallas_call(
        functools.partial(final_kernel, d),
        out_shape=jax.ShapeDtypeStruct((d.rows, d.cols), f32),
        in_specs=[SMEM, VMEM, VMEM, VMEM, VMEM, VMEM],
        out_specs=VMEM,
        scratch_shapes=[
            pltpu.VMEM((2 * d.rows + d.s + 8, d.pw), f32),
            pltpu.VMEM((d.rows, d.pw), f32),
        ],
        compiler_params=limit,
    )(info, summed, ints, divisor, wide_label, row_label)


def solution(mesh):
    in_specs = (
        P(("grp", "con"), ("rep", "sub")),
        P(("grp", "con"), ("rep", "sub")),
        P(("grp", "con")),
        P(("grp", "rep", "sub")),
        P("grp"),
        P("grp"),
    )
    out_specs = P(("grp", "con"), ("rep", "sub"))
    return jax.shard_map(
        per_device, mesh=mesh, in_specs=in_specs, out_specs=out_specs, check_vma=False
    )
```
